32 devices in a mesh: section: 4 (over y, x), dp: 8 (over z, core).
Axes of the slice: x: 2, y: 2, z: 4, core: 2. Of those that a mesh axis runs over, the one named last changes fastest.
Arguments:
- acts: bfloat16 [4, 9, 32, 32, 128], P('section', None, 'dp'), may hold values from -6 to 6
- kernels: bfloat16 [4, 3, 3, 3, 128, 128], P('section'), may hold values from -0.078125 to 0.078125
- cotangent: bfloat16 [9, 32, 32, 128], P(None, 'dp'), may hold values from -6 to 6
Outputs:
- input_grads: bfloat16 [4, 9, 32, 32, 128], P('section', None, 'dp')
- kernel_grads: float32 [4, 128, 27, 128], P('section', 'dp')
The draws below stay inside these ranges and needn't reach their ends.
All inputs are finite; a program needn't handle non-finite values.
Results may differ from the reference program's by a relative error of at most 0.03.
Values may be sent and summed in bfloat16 or wider, within the bound.
A program may use at most 128 MiB of HBM per device.

```python
import math
import jax
import jax.numpy as jnp
from jax import lax

C = 128
F = 9
WIN = 32
H = 32
SECTIONS = 4


def raised(values, stream_key, source, target, parts, factor):
    def block_of(axis_at):
        return (jnp.arange(values.shape[axis_at]) // (values.shape[axis_at] // parts)).reshape((-1,) + (1,) * (values.ndim - 1 - axis_at))

    one_side = jax.random.permutation(stream_key, parts)[block_of(target)]
    other_side = (block_of(target) + parts // 2) % parts
    return jnp.where((block_of(source) == one_side) | (block_of(source) == other_side), factor * values, values)


def level_of(key, extent, shards, low, high):
    factor_of = 1.0
    for axis_at, blocks in shards:
        heights = jax.random.uniform(jax.random.fold_in(jax.random.fold_in(key, 6), axis_at), (blocks,), jnp.float32, low / len(shards), high / len(shards))
        factor_of = factor_of * jnp.repeat(jnp.exp(heights), extent[axis_at] // blocks).reshape((-1,) + (1,) * (len(extent) - 1 - axis_at))
    return factor_of


def normal_values(stream_key, dims, scale, reach, pieces=(), held_as=jnp.bfloat16):
    drawn = scale * jax.random.normal(stream_key, dims, jnp.float32)
    if pieces:
        drawn = drawn * level_of(stream_key, dims, pieces, -0.22, 0.18)
    return jnp.clip(drawn, -reach, reach).astype(held_as)


def heavy_noise(own_key, extent, deviation, reach, cuts, heavy, kind=jnp.bfloat16):
    result = deviation * jax.random.normal(own_key, extent, jnp.float32)
    if cuts:
        result = result * level_of(own_key, extent, cuts, -0.22, 0.18)
    return jnp.clip(raised(result, jax.random.fold_in(own_key, 3), *heavy), -reach, reach).astype(kind)


def setup_inputs(seed: int = 0) -> dict:
    seeds = jax.random.split(jax.random.key(seed), 4)
    acts = heavy_noise(seeds[0], (SECTIONS, F, H, WIN, C), 1.0, 6.0, ((0, 4), (2, 8)), (2, 4, 8, 2.0))
    kernels = normal_values(seeds[1], (SECTIONS, 3, 3, 3, C, C), (54 * C) ** -0.5, 0.078125, ((0, 4),))
    cotangent = normal_values(seeds[2], (F, H, WIN, C), 1.0, 6.0, ((1, 8),))
    return {"acts": acts, "kernels": kernels, "cotangent": cotangent}


def back_conv(kern, grad):
    flipped = jnp.swapaxes(kern[::-1, ::-1, ::-1], 3, 4)
    out = lax.conv_general_dilated(grad[None], flipped, (1, 1, 1), ((0, 2), (1, 1), (1, 1)), dimension_numbers=('NDHWC', 'DHWIO', 'NDHWC'), preferred_element_type=jnp.float32)
    return out[0]

def kernel_term(upad, grad):
    flat = grad.reshape(-1, grad.shape[-1])
    terms = []
    for i in range(3):
        for j in range(3):
            for k in range(3):
                sliced = upad[i:i + F, j:j + H, k:k + WIN].reshape(-1, upad.shape[-1])
                terms.append(jnp.dot(sliced.T, flat, preferred_element_type=jnp.float32))
    return jnp.stack(terms, axis=1)

def reference(acts, kernels, cotangent):
    scale = 1.0 / math.sqrt(F * H * WIN)
    grad = cotangent
    grads_out = []
    kernel_out = []
    for section_id in range(SECTIONS - 1, -1, -1):
        xval = acts[section_id].astype(jnp.float32)
        sig = jax.nn.sigmoid(xval)
        slope = sig * (1.0 + xval * (1.0 - sig))
        back = back_conv(kernels[section_id], grad)
        new_grad = (grad.astype(jnp.float32) + slope * back).astype(jnp.bfloat16)
        activ = (xval * sig).astype(jnp.bfloat16)
        upad = jnp.pad(activ, ((2, 0), (1, 1), (1, 1), (0, 0)))
        kernel_out.append(kernel_term(upad, grad) * scale)
        grads_out.append(new_grad)
        grad = new_grad
    return (jnp.stack(grads_out[::-1], axis=0), jnp.stack(kernel_out[::-1], axis=0))
```

```python
import functools
import math

import jax
import jax.numpy as jnp
from jax import lax
from jax.experimental import pallas as pl
from jax.experimental.pallas import tpu as pltpu
from jax.sharding import PartitionSpec as P

MESH = pl.DeviceIdType.MESH
F32 = jnp.float32
BF16 = jnp.bfloat16


def kernel(
    S, G, step, share,
    acts, kern, cot,
    dx, dw,
    gp, g9, kt, slope, ut, acc, sb, r1, c2, r2,
    main_s, main_r, lo_s, lo_r, hi_s, hi_r, lo_c, hi_c, s1, q1, s2, q2,
):
    F, R, W, C = cot.shape
    Z = G // 2
    n = step
    M = n * R * W
    chunks = F // n
    s = lax.axis_index("section")
    d = lax.axis_index("dp")
    z = d // 2
    core = d % 2
    first = s == S - 1
    prev, nxt = jnp.maximum(s - 1, 0), jnp.minimum(s + 1, S - 1)
    below, above = jnp.maximum(d - 1, 0), jnp.minimum(d + 1, G - 1)
    partner = d + 1 - 2 * core
    has_below, has_above = d > 0, d < G - 1
    has_prev, has_next = s > 0, s < S - 1

    barrier = pltpu.get_barrier_semaphore()

    def greet(sec, dev):
        pl.semaphore_signal(barrier, inc=1, device_id=(sec, dev), device_id_type=MESH)

    def greet_three(sec, own):
        if own:
            greet(sec, d)

        @pl.when(has_below)
        def _():
            greet(sec, below)

        @pl.when(has_above)
        def _():
            greet(sec, above)

    greet_three(s, False)

    @pl.when(has_prev)
    def _():
        greet_three(prev, True)

    @pl.when(has_next)
    def _():
        greet_three(nxt, True)

    for zz in range(Z):
        @pl.when(z != zz)
        def _():
            greet(s, 2 * zz + core)

    ends = has_below.astype(jnp.int32) + has_above.astype(jnp.int32)
    sides = has_prev.astype(jnp.int32) + has_next.astype(jnp.int32)
    pl.semaphore_wait(barrier, ends + sides * (ends + 1) + (Z - 1))

    def rows_copy(q):
        f = pl.ds(q * n, n)
        return pltpu.make_async_remote_copy(
            dx.at[f], gp.at[f, pl.ds(1, R)], main_s.at[q], main_r.at[q],
            device_id=(prev, d), device_id_type=MESH)

    def low_copy(q, source, sec, sent):
        f = pl.ds(q * n, n)
        return pltpu.make_async_remote_copy(
            source.at[f, pl.ds(R - 1, 1)], gp.at[f, pl.ds(0, 1)], sent.at[q], lo_r.at[q],
            device_id=(sec, above), device_id_type=MESH)

    def high_copy(q, source, sec, sent):
        f = pl.ds(q * n, n)
        return pltpu.make_async_remote_copy(
            source.at[f, pl.ds(0, 1)], gp.at[f, pl.ds(R + 1, 1)], sent.at[q], hi_r.at[q],
            device_id=(sec, below), device_id_type=MESH)

    def start_edges(q, source, sec, low_sent, high_sent):
        @pl.when(has_above)
        def _():
            low_copy(q, source, sec, low_sent).start()

        @pl.when(has_below)
        def _():
            high_copy(q, source, sec, high_sent).start()

    order = list(range(chunks))[::-1]

    @pl.when(first)
    def _():
        for q in order:
            start_edges(q, cot, s, lo_c, hi_c)
        gp[pl.ds(0, F), pl.ds(1, R)] = cot[...]

    gp[pl.ds(F, 2)] = jnp.zeros((2, R + 2, W, C), BF16)

    @pl.when(d == 0)
    def _():
        gp[pl.ds(0, F), pl.ds(0, 1)] = jnp.zeros((F, 1, W, C), BF16)

    @pl.when(d == G - 1)
    def _():
        gp[pl.ds(0, F), pl.ds(R + 1, 1)] = jnp.zeros((F, 1, W, C), BF16)

    for i in range(3):
        for j in range(3):
            for k in range(3):
                kt[pl.ds((3 * i + j) * C, C), pl.ds(k * C, C)] = kern[i, j, k].T

    col = lax.rem(lax.broadcasted_iota(jnp.int32, (M, C), 0), W)
    not_first, not_last = col > 0, col < W - 1

    def from_left(v):
        return jnp.where(not_first, pltpu.roll(v, 1, 0), 0.0)

    def from_right(v):
        return jnp.where(not_last, pltpu.roll(v, M - 1, 0), 0.0)

    for q in order:
        x = acts[pl.ds(q * n, n)].reshape(M, C).astype(F32)
        sig = jax.nn.sigmoid(x)
        slope[pl.ds(q * M, M)] = sig * (1.0 + x * (1.0 - sig))
        u = (x * sig).astype(BF16).astype(F32)
        for k, v in enumerate((from_left(u), u, from_right(u))):
            ut[pl.ds(k * C, C), pl.ds(q * M, M)] = v.T.astype(BF16)

    def share_out(i, part):
        for j in range(3):
            for k in range(3):
                block = part[k * C:(k + 1) * C, j * C:(j + 1) * C].astype(BF16)
                if share % 16 == 0:
                    block = block.reshape(Z, 2, share, C)
                    for p in range(2):
                        sb[i, p, :, 3 * j + k] = block[:, p]
                else:
                    for dd in range(G):
                        sb[i, dd % 2, dd // 2, 3 * j + k, pl.ds(0, share)] = (
                            block[dd * share:(dd + 1) * share])

    def pair_copy(i):
        return pltpu.make_async_remote_copy(
            sb.at[i, 1 - core], r1.at[i], s1.at[i], q1.at[i],
            device_id=(s, partner), device_id_type=MESH)

    def chip_copy(i, zz):
        return pltpu.make_async_remote_copy(
            c2.at[i, zz], r2.at[i, z], s2.at[i, zz], q2.at[i, z],
            device_id=(s, 2 * zz + core), device_id_type=MESH)

    def chip_arrival(i, zz):
        return pltpu.make_async_remote_copy(
            c2.at[i, zz], r2.at[i, zz], s2.at[i, zz], q2.at[i, zz],
            device_id=(s, 2 * zz + core), device_id_type=MESH)

    for q in order:
        f = pl.ds(q * n, n)

        @pl.when(has_next)
        def _():
            rows_copy(q).wait_recv()

        @pl.when(has_below)
        def _():
            low_copy(q, dx, prev, lo_s).wait_recv()

        @pl.when(has_above)
        def _():
            high_copy(q, dx, prev, hi_s).wait_recv()

        for i in range(3):
            for j in range(3):
                g9[:, pl.ds((3 * i + j) * C, C)] = gp[
                    pl.ds(q * n + 2 - i, n), pl.ds(2 - j, R)].reshape(M, C)

        parts = jnp.dot(g9[...], kt[...], preferred_element_type=F32)
        back = from_right(parts[:, :C]) + parts[:, C:2 * C] + from_left(parts[:, 2 * C:])
        g = gp[f, pl.ds(1, R)].reshape(M, C).astype(F32)
        dx[f] = (g + slope[pl.ds(q * M, M)] * back).astype(BF16).reshape(n, R, W, C)

        @pl.when(has_prev)
        def _():
            start_edges(q, dx, prev, lo_s, hi_s)
            rows_copy(q).start()

        for i in range(3):
            cols = pl.ds(i * 3 * C, 3 * C)
            term = jnp.dot(ut[:, pl.ds(q * M, M)], g9[:, cols], preferred_element_type=F32)
            if q != order[0]:
                term = acc[:, cols] + term
            if q != order[-1]:
                acc[:, cols] = term
            else:
                share_out(i, term)
                pair_copy(i).start()

    for i in range(3):
        pair_copy(i).wait_recv()
        c2[i] = (sb[i, core].astype(F32) + r1[i].astype(F32)).astype(BF16)
        for zz in range(Z):
            @pl.when(z != zz)
            def _():
                chip_copy(i, zz).start()
        r2[i, z] = c2[i, z]

    for i in range(3):
        for zz in range(Z):
            @pl.when(z != zz)
            def _():
                chip_arrival(i, zz).wait_recv()
        total = r2[i, 0].astype(F32)
        for zz in range(1, Z):
            total = total + r2[i, zz].astype(F32)
        dw[pl.ds(9 * i, 9)] = total

    for i in range(3):
        pair_copy(i).wait_send()
        for zz in range(Z):
            @pl.when(z != zz)
            def _():
                chip_copy(i, zz).wait_send()

    for q in order:
        @pl.when(has_prev)
        def _():
            rows_copy(q).wait_send()

        @pl.when(has_above & has_prev)
        def _():
            low_copy(q, dx, prev, lo_s).wait_send()

        @pl.when(has_below & has_prev)
        def _():
            high_copy(q, dx, prev, hi_s).wait_send()

        @pl.when(has_above & first)
        def _():
            low_copy(q, cot, s, lo_c).wait_send()

        @pl.when(has_below & first)
        def _():
            high_copy(q, cot, s, hi_c).wait_send()


def local(S, G, acts, kernels, cotangent):
    F, R, W, C = cotangent.shape
    share = C // G
    sp = -(-share // 16) * 16
    Z = G // 2
    step = 3 if F % 3 == 0 else 1
    chunks = F // step
    scale = 1.0 / math.sqrt(F * R * G * W)
    dma = pltpu.SemaphoreType.DMA
    dx, dw = pl.pallas_call(
        functools.partial(kernel, S, G, step, share),
        out_shape=(
            jax.ShapeDtypeStruct((F, R, W, C), BF16),
            jax.ShapeDtypeStruct((27, sp, C), F32),
        ),
        in_specs=[pl.BlockSpec(memory_space=pltpu.VMEM)] * 3,
        out_specs=[pl.BlockSpec(memory_space=pltpu.VMEM)] * 2,
        scratch_shapes=[
            pltpu.VMEM((F + 2, R + 2, W, C), BF16),
            pltpu.VMEM((step * R * W, 9 * C), BF16),
            pltpu.VMEM((9 * C, 3 * C), BF16),
            pltpu.VMEM((F * R * W, C), F32),
            pltpu.VMEM((3 * C, F * R * W), BF16),
            pltpu.VMEM((3 * C, 9 * C), F32),
            pltpu.VMEM((3, 2, Z, 9, sp, C), BF16),
            pltpu.VMEM((3, Z, 9, sp, C), BF16),
            pltpu.VMEM((3, Z, 9, sp, C), BF16),
            pltpu.VMEM((3, Z, 9, sp, C), BF16),
            dma((chunks,)), dma((chunks,)), dma((chunks,)), dma((chunks,)),
            dma((chunks,)), dma((chunks,)), dma((chunks,)), dma((chunks,)),
            dma((3,)), dma((3,)), dma((3, Z)), dma((3, Z)),
        ],
        compiler_params=pltpu.CompilerParams(
            collective_id=0, has_side_effects=True, vmem_limit_bytes=48 * 2**20
        ),
        cost_estimate=pl.CostEstimate(
            flops=4 * 27 * F * R * W * C * C, bytes_accessed=4 * 27 * C * C, transcendentals=F * R * W * C
        ),
    )(acts[0], kernels[0], cotangent)
    kernel_part = jnp.transpose(dw[:, :share], (1, 0, 2)) * scale
    return (dx[None], kernel_part[None])


def solution(mesh):
    return jax.shard_map(
        functools.partial(local, mesh.shape["section"], mesh.shape["dp"]),
        mesh=mesh,
        in_specs=(
            P("section", None, "dp", None, None),
            P("section", None, None, None, None, None),
            P(None, "dp", None, None),
        ),
        out_specs=(P("section", None, "dp", None, None), P("section", "dp", None, None)),
        check_vma=False,
    )
```

```python
import functools
import math

import jax
import jax.numpy as jnp
from jax import lax
from jax.experimental import pallas as pl
from jax.experimental.pallas import tpu as pltpu
from jax.sharding import PartitionSpec as P

MESH = pl.DeviceIdType.MESH
F32 = jnp.float32
BF16 = jnp.bfloat16


def kernel(
    S, G, share,
    acts_h, kern_h, cot_h,
    dx, dw,
    acts, kern, gp, g9, kt, slope, ut, acc, sb, r1, c2, r2,
    main_s, main_r, lo_s, lo_r, hi_s, hi_r, edge_s, edge_r, load, s1, q1, s2, q2,
):
    F, R, W, C = cot_h.shape
    Z = G // 2
    M = R * W
    N = 3 * C
    s = lax.axis_index("section")
    d = lax.axis_index("dp")
    z = d // 2
    core = d % 2
    first = s == S - 1
    prev, nxt = jnp.maximum(s - 1, 0), jnp.minimum(s + 1, S - 1)
    below, above = jnp.maximum(d - 1, 0), jnp.minimum(d + 1, G - 1)
    partner = d + 1 - 2 * core
    has_below, has_above = d > 0, d < G - 1
    has_prev, has_next = s > 0, s < S - 1

    acts_load = pltpu.make_async_copy(acts_h, acts, load.at[0])
    kern_load = pltpu.make_async_copy(kern_h, kern, load.at[1])
    cot_load = pltpu.make_async_copy(cot_h, gp.at[:, pl.ds(1, R)], load.at[2])
    acts_load.start()
    kern_load.start()

    @pl.when(first)
    def _():
        cot_load.start()

    barrier = pltpu.get_barrier_semaphore()

    def greet(sec, dev):
        pl.semaphore_signal(barrier, inc=1, device_id=(sec, dev), device_id_type=MESH)

    def greet_three(sec, own):
        if own:
            greet(sec, d)

        @pl.when(has_below)
        def _():
            greet(sec, below)

        @pl.when(has_above)
        def _():
            greet(sec, above)

    greet_three(s, False)

    @pl.when(has_prev)
    def _():
        greet_three(prev, True)

    @pl.when(has_next)
    def _():
        greet_three(nxt, True)

    for zz in range(Z):
        @pl.when(z != zz)
        def _():
            greet(s, 2 * zz + core)

    acts_load.wait()
    for t in range(F):
        x = acts[t].reshape(M, C).astype(F32)
        sig = jax.nn.sigmoid(x)
        slope[t] = sig * (1.0 + x * (1.0 - sig))

    ends = has_below.astype(jnp.int32) + has_above.astype(jnp.int32)
    sides = has_prev.astype(jnp.int32) + has_next.astype(jnp.int32)
    pl.semaphore_wait(barrier, ends + sides * (ends + 1) + (Z - 1))

    def cot_low():
        return pltpu.make_async_remote_copy(
            cot_h.at[:, pl.ds(R - 1, 1)], gp.at[:, pl.ds(0, 1)], edge_s.at[0], edge_r.at[0],
            device_id=(s, above), device_id_type=MESH)

    def cot_high():
        return pltpu.make_async_remote_copy(
            cot_h.at[:, pl.ds(0, 1)], gp.at[:, pl.ds(R + 1, 1)], edge_s.at[1], edge_r.at[1],
            device_id=(s, below), device_id_type=MESH)

    def rows_copy(t):
        return pltpu.make_async_remote_copy(
            dx.at[t], gp.at[t, pl.ds(1, R)], main_s.at[t], main_r.at[t],
            device_id=(prev, d), device_id_type=MESH)

    def low_copy(t):
        return pltpu.make_async_remote_copy(
            dx.at[t, pl.ds(R - 1, 1)], gp.at[t, pl.ds(0, 1)], lo_s.at[t], lo_r.at[t],
            device_id=(prev, above), device_id_type=MESH)

    def high_copy(t):
        return pltpu.make_async_remote_copy(
            dx.at[t, pl.ds(0, 1)], gp.at[t, pl.ds(R + 1, 1)], hi_s.at[t], hi_r.at[t],
            device_id=(prev, below), device_id_type=MESH)

    @pl.when(first & has_above)
    def _():
        cot_low().start()

    @pl.when(first & has_below)
    def _():
        cot_high().start()

    @pl.when(d == 0)
    def _():
        gp[:, pl.ds(0, 1)] = jnp.zeros((F, 1, W, C), BF16)

    @pl.when(d == G - 1)
    def _():
        gp[:, pl.ds(R + 1, 1)] = jnp.zeros((F, 1, W, C), BF16)

    g9[F - 1, :, pl.ds(0, 2 * N)] = jnp.zeros((M, 2 * N), BF16)
    g9[F - 2, :, pl.ds(0, N)] = jnp.zeros((M, N), BF16)

    kern_load.wait()
    for i in range(3):
        for j in range(3):
            for k in range(3):
                kt[pl.ds((3 * i + j) * C, C), pl.ds(k * C, C)] = kern[i, j, k].T

    col = lax.rem(lax.broadcasted_iota(jnp.int32, (M, C), 0), W)
    not_first, not_last = col > 0, col < W - 1

    def from_left(v):
        return jnp.where(not_first, pltpu.roll(v, 1, 0), 0.0)

    def from_right(v):
        return jnp.where(not_last, pltpu.roll(v, M - 1, 0), 0.0)

    def activated():
        for t in range(F):
            x = acts[t].reshape(M, C).astype(F32)
            u = (x * jax.nn.sigmoid(x)).astype(BF16).astype(F32)
            for k, v in enumerate((from_left(u), u, from_right(u))):
                ut[pl.ds(k * C, C), pl.ds(t * M, M)] = v.T.astype(BF16)

    pl.when(has_next)(activated)

    def share_out(i, part):
        for j in range(3):
            for k in range(3):
                block = part[k * C:(k + 1) * C, j * C:(j + 1) * C].astype(BF16)
                if share % 16 == 0:
                    block = block.reshape(Z, 2, share, C)
                    for p in range(2):
                        sb[i, p, :, 3 * j + k] = block[:, p]
                else:
                    for dd in range(G):
                        sb[i, dd % 2, dd // 2, 3 * j + k, pl.ds(0, share)] = (
                            block[dd * share:(dd + 1) * share])

    def pair_copy(i):
        return pltpu.make_async_remote_copy(
            sb.at[i, 1 - core], r1.at[i], s1.at[i], q1.at[i],
            device_id=(s, partner), device_id_type=MESH)

    def chip_copy(i, zz):
        return pltpu.make_async_remote_copy(
            c2.at[i, zz], r2.at[i, z], s2.at[i, zz], q2.at[i, z],
            device_id=(s, 2 * zz + core), device_id_type=MESH)

    def chip_arrival(i, zz):
        return pltpu.make_async_remote_copy(
            c2.at[i, zz], r2.at[i, zz], s2.at[i, zz], q2.at[i, zz],
            device_id=(s, 2 * zz + core), device_id_type=MESH)

    def pair_sum(i):
        pair_copy(i).wait_recv()
        c2[i] = (sb[i, core].astype(F32) + r1[i].astype(F32)).astype(BF16)
        for zz in range(Z):
            @pl.when(z != zz)
            def _():
                chip_copy(i, zz).start()
        r2[i, z] = c2[i, z]

    def conv(t):
        parts = jnp.dot(g9[t], kt[...], preferred_element_type=F32)
        back = from_right(parts[:, :C]) + parts[:, C:2 * C] + from_left(parts[:, 2 * C:])
        g = gp[t, pl.ds(1, R)].reshape(M, C).astype(F32)
        dx[t] = (g + slope[t] * back).astype(BF16).reshape(R, W, C)

    def taps(low, high):
        count = high - low + 1
        g = g9[pl.ds(low, count), :, pl.ds(2 * N, N)].reshape(count * M, N)
        for i in range(3):
            if low + i < 2:
                continue
            term = jnp.dot(
                ut[:, pl.ds((low - 2 + i) * M, count * M)], g, preferred_element_type=F32)
            if high != F - 1:
                term = acc[i] + term
            if low + i > 2:
                acc[i] = term
            else:
                share_out(i, term)
                pair_copy(i).start()

    @pl.when(first)
    def _():
        cot_load.wait()

    @pl.when(first & has_below)
    def _():
        cot_low().wait_recv()

    @pl.when(first & has_above)
    def _():
        cot_high().wait_recv()

    high = F - 1
    for t in range(F - 1, -1, -1):
        @pl.when(has_next)
        def _():
            rows_copy(t).wait_recv()

        @pl.when(has_next & has_below)
        def _():
            low_copy(t).wait_recv()

        @pl.when(has_next & has_above)
        def _():
            high_copy(t).wait_recv()

        for j in range(3):
            piece = gp[t, pl.ds(2 - j, R)].reshape(M, C)
            for i in range(3):
                if t - 2 + i >= 0:
                    g9[t - 2 + i, :, pl.ds((3 * i + j) * C, C)] = piece

        if t > 0:
            conv(t)
        else:
            pl.when(has_prev)(lambda: conv(0))

        @pl.when(has_prev)
        def _():
            rows_copy(t).start()

        @pl.when(has_prev & has_above)
        def _():
            low_copy(t).start()

        @pl.when(has_prev & has_below)
        def _():
            high_copy(t).start()

        if t < 3 or high > t:
            if high == F - 1:
                pl.when(first)(activated)
            taps(t, high)
            high = t - 1
        if t < 2:
            pair_sum(1 - t)

    pair_sum(2)
    pl.when(s == 0)(lambda: conv(0))

    for i in range(3):
        for zz in range(Z):
            @pl.when(z != zz)
            def _():
                chip_arrival(i, zz).wait_recv()
        total = r2[i, 0].astype(F32)
        for zz in range(1, Z):
            total = total + r2[i, zz].astype(F32)
        dw[pl.ds(9 * i, 9)] = total

    for i in range(3):
        pair_copy(i).wait_send()
        for zz in range(Z):
            @pl.when(z != zz)
            def _():
                chip_copy(i, zz).wait_send()

    @pl.when(first & has_above)
    def _():
        cot_low().wait_send()

    @pl.when(first & has_below)
    def _():
        cot_high().wait_send()

    @pl.when(has_prev)
    def _():
        for t in range(F):
            rows_copy(t).wait_send()

    @pl.when(has_prev & has_above)
    def _():
        for t in range(F):
            low_copy(t).wait_send()

    @pl.when(has_prev & has_below)
    def _():
        for t in range(F):
            high_copy(t).wait_send()


def local(S, G, acts, kernels, cotangent):
    F, R, W, C = cotangent.shape
    share = C // G
    sp = -(-share // 16) * 16
    Z = G // 2
    M = R * W
    scale = 1.0 / math.sqrt(F * R * G * W)
    dma = pltpu.SemaphoreType.DMA
    dx, dw = pl.pallas_call(
        functools.partial(kernel, S, G, share),
        out_shape=(
            jax.ShapeDtypeStruct((F, R, W, C), BF16),
            jax.ShapeDtypeStruct((27, sp, C), F32),
        ),
        in_specs=[pl.BlockSpec(memory_space=pltpu.HBM)] * 3,
        out_specs=[pl.BlockSpec(memory_space=pltpu.VMEM)] * 2,
        scratch_shapes=[
            pltpu.VMEM((F, R, W, C), BF16),
            pltpu.VMEM((3, 3, 3, C, C), BF16),
            pltpu.VMEM((F, R + 2, W, C), BF16),
            pltpu.VMEM((F, M, 9 * C), BF16),
            pltpu.VMEM((9 * C, 3 * C), BF16),
            pltpu.VMEM((F, M, C), F32),
            pltpu.VMEM((3 * C, F * M), BF16),
            pltpu.VMEM((3, 3 * C, 3 * C), F32),
            pltpu.VMEM((3, 2, Z, 9, sp, C), BF16),
            pltpu.VMEM((3, Z, 9, sp, C), BF16),
            pltpu.VMEM((3, Z, 9, sp, C), BF16),
            pltpu.VMEM((3, Z, 9, sp, C), BF16),
            dma((F,)), dma((F,)), dma((F,)), dma((F,)), dma((F,)), dma((F,)),
            dma((2,)), dma((2,)), dma((3,)),
            dma((3,)), dma((3,)), dma((3, Z)), dma((3, Z)),
        ],
        compiler_params=pltpu.CompilerParams(
            collective_id=0, has_side_effects=True, vmem_limit_bytes=48 * 2**20
        ),
        cost_estimate=pl.CostEstimate(
            flops=4 * 27 * F * M * C * C, bytes_accessed=4 * 27 * C * C, transcendentals=F * M * C
        ),
    )(acts[0], kernels[0], cotangent)
    kernel_part = jnp.transpose(dw[:, :share], (1, 0, 2)) * scale
    return (dx[None], kernel_part[None])


def solution(mesh):
    return jax.shard_map(
        functools.partial(local, mesh.shape["section"], mesh.shape["dp"]),
        mesh=mesh,
        in_specs=(
            P("section", None, "dp", None, None),
            P("section", None, None, None, None, None),
            P(None, "dp", None, None),
        ),
        out_specs=(P("section", None, "dp", None, None), P("section", "dp", None, None)),
        check_vma=False,
    )
```

```python
import functools
import math

import jax
import jax.numpy as jnp
from jax import lax
from jax.experimental import pallas as pl
from jax.experimental.pallas import tpu as pltpu
from jax.sharding import PartitionSpec as P

MESH = pl.DeviceIdType.MESH
F32 = jnp.float32
BF16 = jnp.bfloat16


def kernel(
    S, G, share,
    acts_h, kern_h, cot_h,
    dx, dw,
    acts, kern, gp, g9, kt, slope, ut, acc, sb, r1, c2, r2,
    main_s, main_r, lo_s, lo_r, hi_s, hi_r, edge_s, edge_r, load, s1, q1, s2, q2,
):
    F, R, W, C = cot_h.shape
    Z = G // 2
    M = R * W
    N = 3 * C
    s = lax.axis_index("section")
    d = lax.axis_index("dp")
    z = d // 2
    core = d % 2
    first = s == S - 1
    prev, nxt = jnp.maximum(s - 1, 0), jnp.minimum(s + 1, S - 1)
    below, above = jnp.maximum(d - 1, 0), jnp.minimum(d + 1, G - 1)
    partner = d + 1 - 2 * core
    has_below, has_above = d > 0, d < G - 1
    has_prev, has_next = s > 0, s < S - 1

    acts_load = pltpu.make_async_copy(acts_h, acts, load.at[0])
    kern_load = pltpu.make_async_copy(kern_h, kern, load.at[1])
    cot_load = pltpu.make_async_copy(cot_h, gp.at[:, pl.ds(1, R)], load.at[2])
    acts_load.start()
    kern_load.start()

    @pl.when(first)
    def _():
        cot_load.start()

    barrier = pltpu.get_barrier_semaphore()

    def greet(sec, dev):
        pl.semaphore_signal(barrier, inc=1, device_id=(sec, dev), device_id_type=MESH)

    def greet_three(sec, own):
        if own:
            greet(sec, d)

        @pl.when(has_below)
        def _():
            greet(sec, below)

        @pl.when(has_above)
        def _():
            greet(sec, above)

    greet_three(s, False)

    @pl.when(has_prev)
    def _():
        greet_three(prev, True)

    @pl.when(has_next)
    def _():
        greet_three(nxt, True)

    for zz in range(Z):
        @pl.when(z != zz)
        def _():
            greet(s, 2 * zz + core)

    acts_load.wait()

    @pl.loop(0, F)
    def _(t):
        x = acts[t].reshape(M, C).astype(F32)
        sig = jax.nn.sigmoid(x)
        slope[t] = sig * (1.0 + x * (1.0 - sig))

    ends = has_below.astype(jnp.int32) + has_above.astype(jnp.int32)
    sides = has_prev.astype(jnp.int32) + has_next.astype(jnp.int32)
    pl.semaphore_wait(barrier, ends + sides * (ends + 1) + (Z - 1))

    def cot_low():
        return pltpu.make_async_remote_copy(
            cot_h.at[:, pl.ds(R - 1, 1)], gp.at[:, pl.ds(0, 1)], edge_s.at[0], edge_r.at[0],
            device_id=(s, above), device_id_type=MESH)

    def cot_high():
        return pltpu.make_async_remote_copy(
            cot_h.at[:, pl.ds(0, 1)], gp.at[:, pl.ds(R + 1, 1)], edge_s.at[1], edge_r.at[1],
            device_id=(s, below), device_id_type=MESH)

    def rows_copy(t):
        return pltpu.make_async_remote_copy(
            dx.at[t], gp.at[t, pl.ds(1, R)], main_s.at[t], main_r.at[t],
            device_id=(prev, d), device_id_type=MESH)

    def low_copy(t):
        return pltpu.make_async_remote_copy(
            dx.at[t, pl.ds(R - 1, 1)], gp.at[t, pl.ds(0, 1)], lo_s.at[t], lo_r.at[t],
            device_id=(prev, above), device_id_type=MESH)

    def high_copy(t):
        return pltpu.make_async_remote_copy(
            dx.at[t, pl.ds(0, 1)], gp.at[t, pl.ds(R + 1, 1)], hi_s.at[t], hi_r.at[t],
            device_id=(prev, below), device_id_type=MESH)

    @pl.when(first & has_above)
    def _():
        cot_low().start()

    @pl.when(first & has_below)
    def _():
        cot_high().start()

    @pl.when(d == 0)
    def _():
        gp[:, pl.ds(0, 1)] = jnp.zeros((F, 1, W, C), BF16)

    @pl.when(d == G - 1)
    def _():
        gp[:, pl.ds(R + 1, 1)] = jnp.zeros((F, 1, W, C), BF16)

    g9[F + 1, :, pl.ds(0, 2 * N)] = jnp.zeros((M, 2 * N), BF16)
    g9[F, :, pl.ds(0, N)] = jnp.zeros((M, N), BF16)

    kern_load.wait()

    @pl.loop(0, 9)
    def _(tap):
        for k in range(3):
            kt[pl.ds(pl.multiple_of(tap * C, C), C), pl.ds(k * C, C)] = kern[tap, k].T

    col = lax.rem(lax.broadcasted_iota(jnp.int32, (M, C), 0), W)
    not_first, not_last = col > 0, col < W - 1

    def from_left(v):
        return jnp.where(not_first, pltpu.roll(v, 1, 0), 0.0)

    def from_right(v):
        return jnp.where(not_last, pltpu.roll(v, M - 1, 0), 0.0)


    def share_out(i, part):
        for j in range(3):
            for k in range(3):
                block = part[k * C:(k + 1) * C, j * C:(j + 1) * C].astype(BF16)
                if share % 16 == 0:
                    block = block.reshape(Z, 2, share, C)
                    for p in range(2):
                        sb[i, p, :, 3 * j + k] = block[:, p]
                else:
                    for dd in range(G):
                        sb[i, dd % 2, dd // 2, 3 * j + k, pl.ds(0, share)] = (
                            block[dd * share:(dd + 1) * share])

    def pair_copy(i):
        return pltpu.make_async_remote_copy(
            sb.at[i, 1 - core], r1.at[i], s1.at[i], q1.at[i],
            device_id=(s, partner), device_id_type=MESH)

    def chip_copy(i, zz):
        return pltpu.make_async_remote_copy(
            c2.at[i, zz], r2.at[i, z], s2.at[i, zz], q2.at[i, z],
            device_id=(s, 2 * zz + core), device_id_type=MESH)

    def chip_arrival(i, zz):
        return pltpu.make_async_remote_copy(
            c2.at[i, zz], r2.at[i, zz], s2.at[i, zz], q2.at[i, zz],
            device_id=(s, 2 * zz + core), device_id_type=MESH)

    def pair_sum(i):
        pair_copy(i).wait_recv()
        c2[i] = (sb[i, core].astype(F32) + r1[i].astype(F32)).astype(BF16)
        for zz in range(Z):
            @pl.when(z != zz)
            def _():
                chip_copy(i, zz).start()
        r2[i, z] = c2[i, z]

    def conv(t):
        parts = jnp.dot(g9[t + 2], kt[...], preferred_element_type=F32)
        back = from_right(parts[:, :C]) + parts[:, C:2 * C] + from_left(parts[:, 2 * C:])
        g = gp[t, pl.ds(1, R)].reshape(M, C).astype(F32)
        dx[t] = (g + slope[t] * back).astype(BF16).reshape(R, W, C)

    def taps(low, count, parts):
        g = g9[pl.ds(low + 2, count), :, pl.ds(2 * N, N)].reshape(count * M, N)
        for i in parts:
            at = low - 2 + i
            u = ut[at] if count == 1 else jnp.concatenate([ut[at], ut[at + 1]], axis=1)
            term = acc[i] + jnp.dot(u, g, preferred_element_type=F32)
            if not isinstance(low, int) or low + i > 2:
                acc[i] = term
            else:
                share_out(i, term)
                pair_copy(i).start()

    def frame(t):
        @pl.when(has_next)
        def _():
            rows_copy(t).wait_recv()

        @pl.when(has_next & has_below)
        def _():
            low_copy(t).wait_recv()

        @pl.when(has_next & has_above)
        def _():
            high_copy(t).wait_recv()

        for j in range(3):
            piece = gp[t, pl.ds(2 - j, R)].reshape(M, C)
            for i in range(3):
                g9[t + i, :, pl.ds((3 * i + j) * C, C)] = piece

        @pl.when((t > 0) | has_prev)
        def _():
            conv(t)

        @pl.when(has_prev)
        def _():
            rows_copy(t).start()

        @pl.when(has_prev & has_above)
        def _():
            low_copy(t).start()

        @pl.when(has_prev & has_below)
        def _():
            high_copy(t).start()

    @pl.when(first)
    def _():
        cot_load.wait()

    @pl.when(first & has_below)
    def _():
        cot_low().wait_recv()

    @pl.when(first & has_above)
    def _():
        cot_high().wait_recv()

    @pl.when(first)
    def _():
        @pl.loop(0, F)
        def _(back_t):
            frame(F - 1 - back_t)

    @pl.loop(0, F)
    def _(t):
        x = acts[t].reshape(M, C).astype(F32)
        u = (x * jax.nn.sigmoid(x)).astype(BF16).astype(F32)
        for k, v in enumerate((from_left(u), u, from_right(u))):
            ut[t, pl.ds(k * C, C)] = v.T.astype(BF16)

    for i in range(3):
        acc[i] = jnp.zeros((N, N), F32)

    @pl.loop(0, F)
    def _(back_t):
        t = F - 1 - back_t

        @pl.when(has_next)
        def _():
            frame(t)

        if F % 2:
            @pl.when((t > 2) & (t % 2 == 1))
            def _():
                taps(t, 2, range(3))
        else:
            @pl.when(t > 2)
            def _():
                taps(t, 1, range(3))

        @pl.when(t == 2)
        def _():
            taps(2, 1, range(3))

        @pl.when(t == 1)
        def _():
            taps(1, 1, (1, 2))
            pair_sum(0)

        @pl.when(t == 0)
        def _():
            taps(0, 1, (2,))
            pair_sum(1)

    pair_sum(2)
    pl.when(s == 0)(lambda: conv(0))

    for i in range(3):
        for zz in range(Z):
            @pl.when(z != zz)
            def _():
                chip_arrival(i, zz).wait_recv()
        total = r2[i, 0].astype(F32)
        for zz in range(1, Z):
            total = total + r2[i, zz].astype(F32)
        dw[pl.ds(9 * i, 9)] = total

    for i in range(3):
        pair_copy(i).wait_send()
        for zz in range(Z):
            @pl.when(z != zz)
            def _():
                chip_copy(i, zz).wait_send()

    @pl.when(first & has_above)
    def _():
        cot_low().wait_send()

    @pl.when(first & has_below)
    def _():
        cot_high().wait_send()

    @pl.when(has_prev)
    def _():
        @pl.loop(0, F)
        def _(t):
            rows_copy(t).wait_send()

    @pl.when(has_prev & has_above)
    def _():
        @pl.loop(0, F)
        def _(t):
            low_copy(t).wait_send()

    @pl.when(has_prev & has_below)
    def _():
        @pl.loop(0, F)
        def _(t):
            high_copy(t).wait_send()


def local(S, G, acts, kernels, cotangent):
    F, R, W, C = cotangent.shape
    share = C // G
    sp = -(-share // 16) * 16
    Z = G // 2
    M = R * W
    scale = 1.0 / math.sqrt(F * R * G * W)
    dma = pltpu.SemaphoreType.DMA
    dx, dw = pl.pallas_call(
        functools.partial(kernel, S, G, share),
        out_shape=(
            jax.ShapeDtypeStruct((F, R, W, C), BF16),
            jax.ShapeDtypeStruct((27, sp, C), F32),
        ),
        in_specs=[pl.BlockSpec(memory_space=pltpu.HBM)] * 3,
        out_specs=[pl.BlockSpec(memory_space=pltpu.VMEM)] * 2,
        scratch_shapes=[
            pltpu.VMEM((F, R, W, C), BF16),
            pltpu.VMEM((9, 3, C, C), BF16),
            pltpu.VMEM((F, R + 2, W, C), BF16),
            pltpu.VMEM((F + 2, M, 9 * C), BF16),
            pltpu.VMEM((9 * C, 3 * C), BF16),
            pltpu.VMEM((F, M, C), F32),
            pltpu.VMEM((F, 3 * C, M), BF16),
            pltpu.VMEM((3, 3 * C, 3 * C), F32),
            pltpu.VMEM((3, 2, Z, 9, sp, C), BF16),
            pltpu.VMEM((3, Z, 9, sp, C), BF16),
            pltpu.VMEM((3, Z, 9, sp, C), BF16),
            pltpu.VMEM((3, Z, 9, sp, C), BF16),
            dma((F,)), dma((F,)), dma((F,)), dma((F,)), dma((F,)), dma((F,)),
            dma((2,)), dma((2,)), dma((3,)),
            dma((3,)), dma((3,)), dma((3, Z)), dma((3, Z)),
        ],
        compiler_params=pltpu.CompilerParams(
            collective_id=0, has_side_effects=True, vmem_limit_bytes=64 * 2**20 - 2**18
        ),
        cost_estimate=pl.CostEstimate(
            flops=4 * 27 * F * M * C * C, bytes_accessed=4 * 27 * C * C, transcendentals=F * M * C
        ),
    )(acts[0], kernels[0].reshape(9, 3, C, C), cotangent)
    kernel_part = jnp.transpose(dw[:, :share], (1, 0, 2)) * scale
    return (dx[None], kernel_part[None])


def solution(mesh):
    return jax.shard_map(
        functools.partial(local, mesh.shape["section"], mesh.shape["dp"]),
        mesh=mesh,
        in_specs=(
            P("section", None, "dp", None, None),
            P("section", None, None, None, None, None),
            P(None, "dp", None, None),
        ),
        out_specs=(P("section", None, "dp", None, None), P("section", "dp", None, None)),
        check_vma=False,
    )
```

```python
import functools
import math

import jax
import jax.numpy as jnp
from jax import lax
from jax.experimental import pallas as pl
from jax.experimental.pallas import tpu as pltpu
from jax.sharding import PartitionSpec as P

MESH = pl.DeviceIdType.MESH
F32 = jnp.float32
BF16 = jnp.bfloat16


def kernel(
    S, G, share, scale,
    acts_h, kern_h, cot_h,
    dx, dw,
    acts, kern, gp, g9, kt, slope, ut, acc, sb, r1, c2, r2,
    main_s, main_r, outer_s, outer_r, inner_s, inner_r, edge_s, edge_r, load, s1, q1, s2, q2,
):
    F, R, W, C = cot_h.shape
    Z = G // 2
    M = R * W
    N = 3 * C
    s = lax.axis_index("section")
    d = lax.axis_index("dp")
    z = d // 2
    core = d % 2
    first = s == S - 1
    prev, nxt = jnp.maximum(s - 1, 0), jnp.minimum(s + 1, S - 1)
    below, above = jnp.maximum(d - 1, 0), jnp.minimum(d + 1, G - 1)
    partner = d + 1 - 2 * core
    has_below, has_above = d > 0, d < G - 1
    outer = jnp.clip(d - 1 + 2 * core, 0, G - 1)
    has_outer = (d + core > 0) & (d + core < G)
    has_prev, has_next = s > 0, s < S - 1

    acts_load = pltpu.make_async_copy(acts_h, acts, load.at[0])
    kern_load = pltpu.make_async_copy(kern_h, kern, load.at[1])
    cot_load = pltpu.make_async_copy(cot_h, gp.at[:, pl.ds(1, R)], load.at[2])
    acts_load.start()
    kern_load.start()

    @pl.when(first)
    def _():
        cot_load.start()

    barrier = pltpu.get_barrier_semaphore()

    def greet(sec, dev):
        pl.semaphore_signal(barrier, inc=1, device_id=(sec, dev), device_id_type=MESH)

    def greet_side(sec):
        greet(sec, d)

        @pl.when(has_outer)
        def _():
            greet(sec, outer)

    greet(s, partner)

    @pl.when(has_outer)
    def _():
        greet(s, outer)

    pl.when(has_prev)(lambda: greet_side(prev))
    pl.when(has_next)(lambda: greet_side(nxt))

    for zz in range(Z):
        @pl.when(z != zz)
        def _():
            greet(s, 2 * zz + core)

    acts_load.wait()

    @pl.loop(0, F)
    def _(t):
        x = acts[t].reshape(M, C).astype(F32)
        sig = jax.nn.sigmoid(x)
        slope[t] = sig * (1.0 + x * (1.0 - sig))

    far = has_outer.astype(jnp.int32)
    sides = has_prev.astype(jnp.int32) + has_next.astype(jnp.int32)
    pl.semaphore_wait(barrier, (1 + far) * (1 + sides) + (Z - 1))

    def cot_low():
        return pltpu.make_async_remote_copy(
            cot_h.at[:, pl.ds(R - 1, 1)], gp.at[:, pl.ds(0, 1)], edge_s.at[0], edge_r.at[0],
            device_id=(s, above), device_id_type=MESH)

    def cot_high():
        return pltpu.make_async_remote_copy(
            cot_h.at[:, pl.ds(0, 1)], gp.at[:, pl.ds(R + 1, 1)], edge_s.at[1], edge_r.at[1],
            device_id=(s, below), device_id_type=MESH)

    def rows_copy(t):
        return pltpu.make_async_remote_copy(
            dx.at[t], gp.at[t, pl.ds(1, R)], main_s.at[t], main_r.at[t],
            device_id=(prev, d), device_id_type=MESH)

    def outer_copy(t):
        return pltpu.make_async_remote_copy(
            dx.at[t, pl.ds(core * (R - 1), 1)], gp.at[t, pl.ds((1 - core) * (R + 1), 1)],
            outer_s.at[t], outer_r.at[t], device_id=(prev, outer), device_id_type=MESH)

    def inner_copy(t):
        return pltpu.make_async_remote_copy(
            gp.at[t, pl.ds(R - core * (R - 1), 1)], gp.at[t, pl.ds(core * (R + 1), 1)],
            inner_s.at[t], inner_r.at[t], device_id=(s, partner), device_id_type=MESH)

    @pl.when(first & has_above)
    def _():
        cot_low().start()

    @pl.when(first & has_below)
    def _():
        cot_high().start()

    @pl.when(d == 0)
    def _():
        gp[:, pl.ds(0, 1)] = jnp.zeros((F, 1, W, C), BF16)

    @pl.when(d == G - 1)
    def _():
        gp[:, pl.ds(R + 1, 1)] = jnp.zeros((F, 1, W, C), BF16)

    g9[F + 1, :, pl.ds(0, 2 * N)] = jnp.zeros((M, 2 * N), BF16)
    g9[F, :, pl.ds(0, N)] = jnp.zeros((M, N), BF16)

    kern_load.wait()

    @pl.loop(0, 9)
    def _(tap):
        for k in range(3):
            kt[pl.ds(pl.multiple_of(tap * C, C), C), pl.ds(k * C, C)] = kern[tap, k].T

    col = lax.rem(lax.broadcasted_iota(jnp.int32, (M, C), 0), W)
    not_first, not_last = col > 0, col < W - 1

    def from_left(v):
        return jnp.where(not_first, pltpu.roll(v, 1, 0), 0.0)

    def from_right(v):
        return jnp.where(not_last, pltpu.roll(v, M - 1, 0), 0.0)


    def share_out(i, part):
        for j in range(3):
            for k in range(3):
                block = part[k * C:(k + 1) * C, j * C:(j + 1) * C].astype(BF16)
                if share % 16 == 0:
                    block = block.reshape(Z, 2, share, C)
                    for p in range(2):
                        sb[i, p, :, 3 * j + k] = block[:, p]
                else:
                    for dd in range(G):
                        sb[i, dd % 2, dd // 2, 3 * j + k, pl.ds(0, share)] = (
                            block[dd * share:(dd + 1) * share])

    def pair_copy(i):
        return pltpu.make_async_remote_copy(
            sb.at[i, 1 - core], r1.at[i], s1.at[i], q1.at[i],
            device_id=(s, partner), device_id_type=MESH)

    def chip_copy(i, zz):
        return pltpu.make_async_remote_copy(
            c2.at[i, zz], r2.at[i, z], s2.at[i, zz], q2.at[i, z],
            device_id=(s, 2 * zz + core), device_id_type=MESH)

    def chip_arrival(i, zz):
        return pltpu.make_async_remote_copy(
            c2.at[i, zz], r2.at[i, zz], s2.at[i, zz], q2.at[i, zz],
            device_id=(s, 2 * zz + core), device_id_type=MESH)

    def pair_sum(i):
        pair_copy(i).wait_recv()
        c2[i] = (sb[i, core].astype(F32) + r1[i].astype(F32)).astype(BF16)
        for zz in range(Z):
            @pl.when(z != zz)
            def _():
                chip_copy(i, zz).start()
        r2[i, z] = c2[i, z]

    def conv(t):
        parts = jnp.dot(g9[t + 2], kt[...], preferred_element_type=F32)
        back = from_right(parts[:, :C]) + parts[:, C:2 * C] + from_left(parts[:, 2 * C:])
        g = gp[t, pl.ds(1, R)].reshape(M, C).astype(F32)
        dx[t] = (g + slope[t] * back).astype(BF16).reshape(R, W, C)

    def taps(low, count, parts):
        g = g9[pl.ds(low + 2, count), :, pl.ds(2 * N, N)].reshape(count * M, N)
        for i in parts:
            at = low - 2 + i
            u = ut[at] if count == 1 else jnp.concatenate([ut[at], ut[at + 1]], axis=1)
            term = acc[i] + jnp.dot(u, g, preferred_element_type=F32)
            if not isinstance(low, int) or low + i > 2:
                acc[i] = term
            else:
                share_out(i, term)
                pair_copy(i).start()

    def frame(t):
        @pl.when(has_next)
        def _():
            rows_copy(t).wait_recv()
            inner_copy(t).start()

        @pl.when(has_next & has_outer)
        def _():
            outer_copy(t).wait_recv()

        @pl.when(has_next)
        def _():
            inner_copy(t).wait_recv()

        for j in range(3):
            piece = gp[t, pl.ds(2 - j, R)].reshape(M, C)
            for i in range(3):
                g9[t + i, :, pl.ds((3 * i + j) * C, C)] = piece

        @pl.when((t > 0) | has_prev)
        def _():
            conv(t)

        @pl.when(has_prev & has_outer)
        def _():
            outer_copy(t).start()

        @pl.when(has_prev)
        def _():
            rows_copy(t).start()

    @pl.when(first)
    def _():
        cot_load.wait()

    @pl.when(first & has_below)
    def _():
        cot_low().wait_recv()

    @pl.when(first & has_above)
    def _():
        cot_high().wait_recv()

    @pl.when(first)
    def _():
        @pl.loop(0, F)
        def _(back_t):
            frame(F - 1 - back_t)

    @pl.loop(0, F)
    def _(t):
        x = acts[t].reshape(M, C).astype(F32)
        u = (x * jax.nn.sigmoid(x)).astype(BF16).astype(F32)
        for k, v in enumerate((from_left(u), u, from_right(u))):
            ut[t, pl.ds(k * C, C)] = v.T.astype(BF16)

    for i in range(3):
        acc[i] = jnp.zeros((N, N), F32)

    @pl.loop(0, F)
    def _(back_t):
        t = F - 1 - back_t

        @pl.when(has_next)
        def _():
            frame(t)

        if F % 2:
            @pl.when((t > 2) & (t % 2 == 1))
            def _():
                taps(t, 2, range(3))
        else:
            @pl.when(t > 2)
            def _():
                taps(t, 1, range(3))

        @pl.when(t == 2)
        def _():
            taps(2, 1, range(3))

        @pl.when(t == 1)
        def _():
            taps(1, 1, (1, 2))
            pair_sum(0)

        @pl.when(t == 0)
        def _():
            taps(0, 1, (2,))
            pair_sum(1)

    pair_sum(2)
    pl.when(s == 0)(lambda: conv(0))

    for i in range(3):
        for zz in range(Z):
            @pl.when(z != zz)
            def _():
                chip_arrival(i, zz).wait_recv()
        total = r2[i, 0].astype(F32)
        for zz in range(1, Z):
            total = total + r2[i, zz].astype(F32)
        dw[pl.ds(9 * i, 9)] = total * scale

    for i in range(3):
        pair_copy(i).wait_send()
        for zz in range(Z):
            @pl.when(z != zz)
            def _():
                chip_copy(i, zz).wait_send()

    @pl.when(first & has_above)
    def _():
        cot_low().wait_send()

    @pl.when(first & has_below)
    def _():
        cot_high().wait_send()

    @pl.when(has_prev)
    def _():
        @pl.loop(0, F)
        def _(t):
            rows_copy(t).wait_send()

    @pl.when(has_prev & has_outer)
    def _():
        @pl.loop(0, F)
        def _(t):
            outer_copy(t).wait_send()

    @pl.when(has_next)
    def _():
        @pl.loop(0, F)
        def _(t):
            inner_copy(t).wait_send()


def local(S, G, acts, kernels, cotangent):
    F, R, W, C = cotangent.shape
    share = C // G
    sp = -(-share // 16) * 16
    Z = G // 2
    M = R * W
    scale = 1.0 / math.sqrt(F * R * G * W)
    dma = pltpu.SemaphoreType.DMA
    dx, dw = pl.pallas_call(
        functools.partial(kernel, S, G, share, scale),
        out_shape=(
            jax.ShapeDtypeStruct((F, R, W, C), BF16),
            jax.ShapeDtypeStruct((27, sp, C), F32),
        ),
        in_specs=[pl.BlockSpec(memory_space=pltpu.HBM)] * 3,
        out_specs=[pl.BlockSpec(memory_space=pltpu.VMEM)] * 2,
        scratch_shapes=[
            pltpu.VMEM((F, R, W, C), BF16),
            pltpu.VMEM((9, 3, C, C), BF16),
            pltpu.VMEM((F, R + 2, W, C), BF16),
            pltpu.VMEM((F + 2, M, 9 * C), BF16),
            pltpu.VMEM((9 * C, 3 * C), BF16),
            pltpu.VMEM((F, M, C), F32),
            pltpu.VMEM((F, 3 * C, M), BF16),
            pltpu.VMEM((3, 3 * C, 3 * C), F32),
            pltpu.VMEM((3, 2, Z, 9, sp, C), BF16),
            pltpu.VMEM((3, Z, 9, sp, C), BF16),
            pltpu.VMEM((3, Z, 9, sp, C), BF16),
            pltpu.VMEM((3, Z, 9, sp, C), BF16),
            dma((F,)), dma((F,)), dma((F,)), dma((F,)), dma((F,)), dma((F,)),
            dma((2,)), dma((2,)), dma((3,)),
            dma((3,)), dma((3,)), dma((3, Z)), dma((3, Z)),
        ],
        compiler_params=pltpu.CompilerParams(
            collective_id=0, has_side_effects=True, vmem_limit_bytes=64 * 2**20 - 2**18
        ),
        cost_estimate=pl.CostEstimate(
            flops=4 * 27 * F * M * C * C, bytes_accessed=4 * 27 * C * C, transcendentals=F * M * C
        ),
    )(acts[0], kernels[0].reshape(9, 3, C, C), cotangent)
    kernel_part = jnp.transpose(dw[:, :share], (1, 0, 2))
    return (dx[None], kernel_part[None])


def solution(mesh):
    return jax.shard_map(
        functools.partial(local, mesh.shape["section"], mesh.shape["dp"]),
        mesh=mesh,
        in_specs=(
            P("section", None, "dp", None, None),
            P("section", None, None, None, None, None),
            P(None, "dp", None, None),
        ),
        out_specs=(P("section", None, "dp", None, None), P("section", "dp", None, None)),
        check_vma=False,
    )
```

```python
import functools
import math

import jax
import jax.numpy as jnp
from jax import lax
from jax.experimental import pallas as pl
from jax.experimental.pallas import tpu as pltpu
from jax.sharding import PartitionSpec as P

MESH = pl.DeviceIdType.MESH
F32 = jnp.float32
BF16 = jnp.bfloat16


def kernel(
    S, G, share,
    acts_h, kern_h, cot_h,
    dx, dw,
    acts, kern, gp, g9, kt, slope, ut, acc, sb, r1, c2, r2,
    main_s, main_r, lo_s, lo_r, hi_s, hi_r, edge_s, edge_r, load, s1, q1, s2, q2,
):
    F, R, W, C = cot_h.shape
    Z = G // 2
    M = R * W
    N = 3 * C
    s = lax.axis_index("section")
    d = lax.axis_index("dp")
    z = d // 2
    core = d % 2
    first = s == S - 1
    prev, nxt = jnp.maximum(s - 1, 0), jnp.minimum(s + 1, S - 1)
    below, above = jnp.maximum(d - 1, 0), jnp.minimum(d + 1, G - 1)
    partner = d + 1 - 2 * core
    has_below, has_above = d > 0, d < G - 1
    has_prev, has_next = s > 0, s < S - 1

    acts_load = pltpu.make_async_copy(acts_h, acts, load.at[0])
    kern_load = pltpu.make_async_copy(kern_h, kern, load.at[1])
    cot_load = pltpu.make_async_copy(cot_h, gp.at[:, pl.ds(1, R)], load.at[2])
    acts_load.start()
    kern_load.start()

    @pl.when(first)
    def _():
        cot_load.start()

    barrier = pltpu.get_barrier_semaphore()

    def greet(sec, dev):
        pl.semaphore_signal(barrier, inc=1, device_id=(sec, dev), device_id_type=MESH)

    def greet_three(sec, own):
        if own:
            greet(sec, d)

        @pl.when(has_below)
        def _():
            greet(sec, below)

        @pl.when(has_above)
        def _():
            greet(sec, above)

    greet_three(s, False)

    @pl.when(has_prev)
    def _():
        greet_three(prev, True)

    @pl.when(has_next)
    def _():
        greet_three(nxt, True)

    for zz in range(Z):
        @pl.when(z != zz)
        def _():
            greet(s, 2 * zz + core)

    acts_load.wait()

    @pl.loop(0, F)
    def _(t):
        x = acts[t].reshape(M, C).astype(F32)
        sig = jax.nn.sigmoid(x)
        slope[t] = sig * (1.0 + x * (1.0 - sig))

    ends = has_below.astype(jnp.int32) + has_above.astype(jnp.int32)
    sides = has_prev.astype(jnp.int32) + has_next.astype(jnp.int32)
    pl.semaphore_wait(barrier, ends + sides * (ends + 1) + (Z - 1))

    def cot_low():
        return pltpu.make_async_remote_copy(
            cot_h.at[:, pl.ds(R - 1, 1)], gp.at[:, pl.ds(0, 1)], edge_s.at[0], edge_r.at[0],
            device_id=(s, above), device_id_type=MESH)

    def cot_high():
        return pltpu.make_async_remote_copy(
            cot_h.at[:, pl.ds(0, 1)], gp.at[:, pl.ds(R + 1, 1)], edge_s.at[1], edge_r.at[1],
            device_id=(s, below), device_id_type=MESH)

    def rows_copy(t):
        return pltpu.make_async_remote_copy(
            dx.at[t], gp.at[t, pl.ds(1, R)], main_s.at[t], main_r.at[t],
            device_id=(prev, d), device_id_type=MESH)

    def low_copy(t):
        return pltpu.make_async_remote_copy(
            dx.at[t, pl.ds(R - 1, 1)], gp.at[t, pl.ds(0, 1)], lo_s.at[t], lo_r.at[t],
            device_id=(prev, above), device_id_type=MESH)

    def high_copy(t):
        return pltpu.make_async_remote_copy(
            dx.at[t, pl.ds(0, 1)], gp.at[t, pl.ds(R + 1, 1)], hi_s.at[t], hi_r.at[t],
            device_id=(prev, below), device_id_type=MESH)

    @pl.when(first & has_above)
    def _():
        cot_low().start()

    @pl.when(first & has_below)
    def _():
        cot_high().start()

    @pl.when(d == 0)
    def _():
        gp[:, pl.ds(0, 1)] = jnp.zeros((F, 1, W, C), BF16)

    @pl.when(d == G - 1)
    def _():
        gp[:, pl.ds(R + 1, 1)] = jnp.zeros((F, 1, W, C), BF16)

    g9[F + 1, :, pl.ds(0, 2 * N)] = jnp.zeros((M, 2 * N), BF16)
    g9[F, :, pl.ds(0, N)] = jnp.zeros((M, N), BF16)

    kern_load.wait()

    @pl.loop(0, 9)
    def _(tap):
        for k in range(3):
            kt[pl.ds(pl.multiple_of(tap * C, C), C), pl.ds(k * C, C)] = kern[tap, k].T

    def column(v):
        return lax.rem(lax.broadcasted_iota(jnp.int32, v.shape, 0), W)

    def from_left(v):
        return jnp.where(column(v) > 0, pltpu.roll(v, 1, 0), 0.0)

    def from_right(v):
        return jnp.where(column(v) < W - 1, pltpu.roll(v, v.shape[0] - 1, 0), 0.0)


    def share_out(i, part):
        for j in range(3):
            for k in range(3):
                block = part[k * C:(k + 1) * C, j * C:(j + 1) * C].astype(BF16)
                if share % 16 == 0:
                    block = block.reshape(Z, 2, share, C)
                    for p in range(2):
                        sb[i, p, :, 3 * j + k] = block[:, p]
                else:
                    for dd in range(G):
                        sb[i, dd % 2, dd // 2, 3 * j + k, pl.ds(0, share)] = (
                            block[dd * share:(dd + 1) * share])

    def pair_copy(i):
        return pltpu.make_async_remote_copy(
            sb.at[i, 1 - core], r1.at[i], s1.at[i], q1.at[i],
            device_id=(s, partner), device_id_type=MESH)

    def chip_copy(i, zz):
        return pltpu.make_async_remote_copy(
            c2.at[i, zz], r2.at[i, z], s2.at[i, zz], q2.at[i, z],
            device_id=(s, 2 * zz + core), device_id_type=MESH)

    def chip_arrival(i, zz):
        return pltpu.make_async_remote_copy(
            c2.at[i, zz], r2.at[i, zz], s2.at[i, zz], q2.at[i, zz],
            device_id=(s, 2 * zz + core), device_id_type=MESH)

    def pair_sum(i):
        pair_copy(i).wait_recv()
        c2[i] = (sb[i, core].astype(F32) + r1[i].astype(F32)).astype(BF16)
        for zz in range(Z):
            @pl.when(z != zz)
            def _():
                chip_copy(i, zz).start()
        r2[i, z] = c2[i, z]

    def conv(t, count):
        f, L = pl.ds(t, count), count * M
        parts = jnp.dot(
            g9[pl.ds(t + 2, count)].reshape(L, 9 * C), kt[...], preferred_element_type=F32)
        back = from_right(parts[:, :C]) + parts[:, C:2 * C] + from_left(parts[:, 2 * C:])
        g = gp[f, pl.ds(1, R)].reshape(L, C).astype(F32)
        dx[f] = (g + slope[f].reshape(L, C) * back).astype(BF16).reshape(count, R, W, C)

    def taps(low, count, parts):
        g = g9[pl.ds(low + 2, count), :, pl.ds(2 * N, N)].reshape(count * M, N)
        for i in parts:
            at = low - 2 + i
            u = ut[at] if count == 1 else jnp.concatenate([ut[at], ut[at + 1]], axis=1)
            term = acc[i] + jnp.dot(u, g, preferred_element_type=F32)
            if not isinstance(low, int) or low + i > 2:
                acc[i] = term
            else:
                share_out(i, term)
                pair_copy(i).start()

    def frame(t, chain):
        @pl.when(has_next)
        def _():
            rows_copy(t).wait_recv()

        @pl.when(has_next & has_below)
        def _():
            low_copy(t).wait_recv()

        @pl.when(has_next & has_above)
        def _():
            high_copy(t).wait_recv()

        for j in range(3):
            piece = gp[t, pl.ds(2 - j, R)].reshape(M, C)
            for i in range(3):
                g9[t + i, :, pl.ds((3 * i + j) * C, C)] = piece

        if not chain:
            return
        conv(t, 1)

        @pl.when(has_prev & has_above)
        def _():
            low_copy(t).start()

        @pl.when(has_prev & has_below)
        def _():
            high_copy(t).start()

        @pl.when(has_prev)
        def _():
            rows_copy(t).start()

    def activated():
        @pl.loop(0, F)
        def _(t):
            x = acts[t].reshape(M, C).astype(F32)
            u = (x * jax.nn.sigmoid(x)).astype(BF16).astype(F32)
            for k, v in enumerate((from_left(u), u, from_right(u))):
                ut[t, pl.ds(k * C, C)] = v.T.astype(BF16)

        for i in range(3):
            acc[i] = jnp.zeros((N, N), F32)

    pl.when(has_next)(activated)

    @pl.when(first)
    def _():
        cot_load.wait()

    @pl.when(first & has_below)
    def _():
        cot_low().wait_recv()

    @pl.when(first & has_above)
    def _():
        cot_high().wait_recv()

    @pl.when(has_prev)
    def _():
        @pl.loop(0, F)
        def _(back_t):
            frame(F - 1 - back_t, True)

    pl.when(first)(activated)

    @pl.loop(0, F)
    def _(back_t):
        t = F - 1 - back_t

        @pl.when(s == 0)
        def _():
            frame(t, False)

        if F % 2:
            @pl.when((t > 2) & (t % 2 == 1))
            def _():
                taps(t, 2, range(3))
        else:
            @pl.when(t > 2)
            def _():
                taps(t, 1, range(3))

        @pl.when(t == 2)
        def _():
            taps(2, 1, range(3))

        @pl.when(t == 1)
        def _():
            taps(1, 1, (1, 2))
            pair_sum(0)

        @pl.when(t == 0)
        def _():
            taps(0, 1, (2,))
            pair_sum(1)

    pair_sum(2)

    @pl.when(s == 0)
    def _():
        count = 3 if F % 3 == 0 else 1

        @pl.loop(0, F // count)
        def _(q):
            conv(q * count, count)


    for i in range(3):
        for zz in range(Z):
            @pl.when(z != zz)
            def _():
                chip_arrival(i, zz).wait_recv()
        total = r2[i, 0].astype(F32)
        for zz in range(1, Z):
            total = total + r2[i, zz].astype(F32)
        dw[pl.ds(9 * i, 9)] = total

    for i in range(3):
        pair_copy(i).wait_send()
        for zz in range(Z):
            @pl.when(z != zz)
            def _():
                chip_copy(i, zz).wait_send()

    @pl.when(first & has_above)
    def _():
        cot_low().wait_send()

    @pl.when(first & has_below)
    def _():
        cot_high().wait_send()

    @pl.when(has_prev)
    def _():
        @pl.loop(0, F)
        def _(t):
            rows_copy(t).wait_send()

    @pl.when(has_prev & has_above)
    def _():
        @pl.loop(0, F)
        def _(t):
            low_copy(t).wait_send()

    @pl.when(has_prev & has_below)
    def _():
        @pl.loop(0, F)
        def _(t):
            high_copy(t).wait_send()


def local(S, G, acts, kernels, cotangent):
    F, R, W, C = cotangent.shape
    share = C // G
    sp = -(-share // 16) * 16
    Z = G // 2
    M = R * W
    scale = 1.0 / math.sqrt(F * R * G * W)
    dma = pltpu.SemaphoreType.DMA
    dx, dw = pl.pallas_call(
        functools.partial(kernel, S, G, share),
        out_shape=(
            jax.ShapeDtypeStruct((F, R, W, C), BF16),
            jax.ShapeDtypeStruct((27, sp, C), F32),
        ),
        in_specs=[pl.BlockSpec(memory_space=pltpu.HBM)] * 3,
        out_specs=[pl.BlockSpec(memory_space=pltpu.VMEM)] * 2,
        scratch_shapes=[
            pltpu.VMEM((F, R, W, C), BF16),
            pltpu.VMEM((9, 3, C, C), BF16),
            pltpu.VMEM((F, R + 2, W, C), BF16),
            pltpu.VMEM((F + 2, M, 9 * C), BF16),
            pltpu.VMEM((9 * C, 3 * C), BF16),
            pltpu.VMEM((F, M, C), F32),
            pltpu.VMEM((F, 3 * C, M), BF16),
            pltpu.VMEM((3, 3 * C, 3 * C), F32),
            pltpu.VMEM((3, 2, Z, 9, sp, C), BF16),
            pltpu.VMEM((3, Z, 9, sp, C), BF16),
            pltpu.VMEM((3, Z, 9, sp, C), BF16),
            pltpu.VMEM((3, Z, 9, sp, C), BF16),
            dma((F,)), dma((F,)), dma((F,)), dma((F,)), dma((F,)), dma((F,)),
            dma((2,)), dma((2,)), dma((3,)),
            dma((3,)), dma((3,)), dma((3, Z)), dma((3, Z)),
        ],
        compiler_params=pltpu.CompilerParams(
            collective_id=0, has_side_effects=True, vmem_limit_bytes=64 * 2**20 - 2**18
        ),
        cost_estimate=pl.CostEstimate(
            flops=4 * 27 * F * M * C * C, bytes_accessed=4 * 27 * C * C, transcendentals=F * M * C
        ),
    )(acts[0], kernels[0].reshape(9, 3, C, C), cotangent)
    kernel_part = jnp.transpose(dw[:, :share], (1, 0, 2)) * scale
    return (dx[None], kernel_part[None])


def solution(mesh):
    return jax.shard_map(
        functools.partial(local, mesh.shape["section"], mesh.shape["dp"]),
        mesh=mesh,
        in_specs=(
            P("section", None, "dp", None, None),
            P("section", None, None, None, None, None),
            P(None, "dp", None, None),
        ),
        out_specs=(P("section", None, "dp", None, None), P("section", "dp", None, None)),
        check_vma=False,
    )
```

```python
import functools
import math

import jax
import jax.numpy as jnp
from jax import lax
from jax.experimental import pallas as pl
from jax.experimental.pallas import tpu as pltpu
from jax.sharding import PartitionSpec as P

MESH = pl.DeviceIdType.MESH
F32 = jnp.float32
BF16 = jnp.bfloat16


def kernel(
    S, G, share,
    acts_h, kern_h, cot_h,
    dx, dw,
    acts, kern, gp, g9, kt, slope, ut, acc, sb, r1, c2, r2,
    main_s, main_r, lo_s, lo_r, hi_s, hi_r, edge_s, edge_r, load, s1, q1, s2, q2,
):
    F, R, W, C = cot_h.shape
    Z = G // 2
    M = R * W
    N = 3 * C
    s = lax.axis_index("section")
    d = lax.axis_index("dp")
    z = d // 2
    core = d % 2
    first = s == S - 1
    prev, nxt = jnp.maximum(s - 1, 0), jnp.minimum(s + 1, S - 1)
    below, above = jnp.maximum(d - 1, 0), jnp.minimum(d + 1, G - 1)
    partner = d + 1 - 2 * core
    has_below, has_above = d > 0, d < G - 1
    has_prev, has_next = s > 0, s < S - 1

    acts_load = pltpu.make_async_copy(acts_h, acts, load.at[0])
    kern_load = pltpu.make_async_copy(kern_h, kern, load.at[1])
    cot_load = pltpu.make_async_copy(cot_h, gp.at[:, pl.ds(1, R)], load.at[2])
    acts_load.start()
    kern_load.start()

    @pl.when(first)
    def _():
        cot_load.start()

    barrier = pltpu.get_barrier_semaphore()

    def greet(sec, dev):
        pl.semaphore_signal(barrier, inc=1, device_id=(sec, dev), device_id_type=MESH)

    def greet_three(sec, own):
        if own:
            greet(sec, d)

        @pl.when(has_below)
        def _():
            greet(sec, below)

        @pl.when(has_above)
        def _():
            greet(sec, above)

    greet_three(s, False)

    @pl.when(has_prev)
    def _():
        greet_three(prev, True)

    @pl.when(has_next)
    def _():
        greet_three(nxt, True)

    for zz in range(Z):
        @pl.when(z != zz)
        def _():
            greet(s, 2 * zz + core)

    acts_load.wait()

    @pl.loop(0, F)
    def _(t):
        x = acts[t].reshape(M, C).astype(F32)
        sig = jax.nn.sigmoid(x)
        slope[t] = sig * (1.0 + x * (1.0 - sig))

    ends = has_below.astype(jnp.int32) + has_above.astype(jnp.int32)
    sides = has_prev.astype(jnp.int32) + has_next.astype(jnp.int32)
    pl.semaphore_wait(barrier, ends + sides * (ends + 1) + (Z - 1))

    def cot_low():
        return pltpu.make_async_remote_copy(
            cot_h.at[:, pl.ds(R - 1, 1)], gp.at[:, pl.ds(0, 1)], edge_s.at[0], edge_r.at[0],
            device_id=(s, above), device_id_type=MESH)

    def cot_high():
        return pltpu.make_async_remote_copy(
            cot_h.at[:, pl.ds(0, 1)], gp.at[:, pl.ds(R + 1, 1)], edge_s.at[1], edge_r.at[1],
            device_id=(s, below), device_id_type=MESH)

    def rows_copy(t):
        return pltpu.make_async_remote_copy(
            dx.at[t], gp.at[t, pl.ds(1, R)], main_s.at[t], main_r.at[t],
            device_id=(prev, d), device_id_type=MESH)

    def low_copy(t):
        return pltpu.make_async_remote_copy(
            dx.at[t, pl.ds(R - 1, 1)], gp.at[t, pl.ds(0, 1)], lo_s.at[t], lo_r.at[t],
            device_id=(prev, above), device_id_type=MESH)

    def high_copy(t):
        return pltpu.make_async_remote_copy(
            dx.at[t, pl.ds(0, 1)], gp.at[t, pl.ds(R + 1, 1)], hi_s.at[t], hi_r.at[t],
            device_id=(prev, below), device_id_type=MESH)

    @pl.when(first & has_above)
    def _():
        cot_low().start()

    @pl.when(first & has_below)
    def _():
        cot_high().start()

    @pl.when(d == 0)
    def _():
        gp[:, pl.ds(0, 1)] = jnp.zeros((F, 1, W, C), BF16)

    @pl.when(d == G - 1)
    def _():
        gp[:, pl.ds(R + 1, 1)] = jnp.zeros((F, 1, W, C), BF16)

    g9[F + 1, :, pl.ds(0, 2 * N)] = jnp.zeros((M, 2 * N), BF16)
    g9[F, :, pl.ds(0, N)] = jnp.zeros((M, N), BF16)

    kern_load.wait()

    @pl.loop(0, 9)
    def _(tap):
        for k in range(3):
            kt[pl.ds(pl.multiple_of(tap * C, C), C), pl.ds(k * C, C)] = kern[tap, k].T

    def column(v):
        return lax.rem(lax.broadcasted_iota(jnp.int32, v.shape, 0), W)

    def from_left(v):
        return jnp.where(column(v) > 0, pltpu.roll(v, 1, 0), 0.0)

    def from_right(v):
        return jnp.where(column(v) < W - 1, pltpu.roll(v, v.shape[0] - 1, 0), 0.0)


    def share_out(i, part):
        for j in range(3):
            for k in range(3):
                block = part[k * C:(k + 1) * C, j * C:(j + 1) * C].astype(BF16)
                if share % 16 == 0:
                    block = block.reshape(Z, 2, share, C)
                    for p in range(2):
                        sb[i, p, :, 3 * j + k] = block[:, p]
                else:
                    for dd in range(G):
                        sb[i, dd % 2, dd // 2, 3 * j + k, pl.ds(0, share)] = (
                            block[dd * share:(dd + 1) * share])

    def pair_copy(i):
        return pltpu.make_async_remote_copy(
            sb.at[i, 1 - core], r1.at[i], s1.at[i], q1.at[i],
            device_id=(s, partner), device_id_type=MESH)

    def chip_copy(i, zz):
        return pltpu.make_async_remote_copy(
            c2.at[i, zz], r2.at[i, z], s2.at[i, zz], q2.at[i, z],
            device_id=(s, 2 * zz + core), device_id_type=MESH)

    def chip_arrival(i, zz):
        return pltpu.make_async_remote_copy(
            c2.at[i, zz], r2.at[i, zz], s2.at[i, zz], q2.at[i, zz],
            device_id=(s, 2 * zz + core), device_id_type=MESH)

    def pair_sum(i):
        pair_copy(i).wait_recv()
        c2[i] = (sb[i, core].astype(F32) + r1[i].astype(F32)).astype(BF16)
        for zz in range(Z):
            @pl.when(z != zz)
            def _():
                chip_copy(i, zz).start()
        r2[i, z] = c2[i, z]

    def conv(t, count):
        f, L = pl.ds(t, count), count * M
        parts = jnp.dot(
            g9[pl.ds(t + 2, count)].reshape(L, 9 * C), kt[...], preferred_element_type=F32)
        back = from_right(parts[:, :C]) + parts[:, C:2 * C] + from_left(parts[:, 2 * C:])
        g = gp[f, pl.ds(1, R)].reshape(L, C).astype(F32)
        dx[f] = (g + slope[f].reshape(L, C) * back).astype(BF16).reshape(count, R, W, C)

    def taps(low, count, parts):
        g = g9[pl.ds(low + 2, count), :, pl.ds(2 * N, N)].reshape(count * M, N)
        for i in parts:
            at = low - 2 + i
            u = ut[at] if count == 1 else jnp.concatenate([ut[at], ut[at + 1]], axis=1)
            term = acc[i] + jnp.dot(u, g, preferred_element_type=F32)
            if not isinstance(low, int) or low + i > 2:
                acc[i] = term
            else:
                share_out(i, term)
                pair_copy(i).start()

    def arrive(t):
        @pl.when(has_next)
        def _():
            rows_copy(t).wait_recv()

        @pl.when(has_next & has_below)
        def _():
            low_copy(t).wait_recv()

        @pl.when(has_next & has_above)
        def _():
            high_copy(t).wait_recv()

        for j in range(3):
            piece = gp[t, pl.ds(2 - j, R)].reshape(M, C)
            for i in range(3):
                g9[t + i, :, pl.ds((3 * i + j) * C, C)] = piece

    def send(t):

        @pl.when(has_prev & has_above)
        def _():
            low_copy(t).start()

        @pl.when(has_prev & has_below)
        def _():
            high_copy(t).start()

        @pl.when(has_prev)
        def _():
            rows_copy(t).start()

    def activated():
        @pl.loop(0, F)
        def _(t):
            x = acts[t].reshape(M, C).astype(F32)
            u = (x * jax.nn.sigmoid(x)).astype(BF16).astype(F32)
            for k, v in enumerate((from_left(u), u, from_right(u))):
                ut[t, pl.ds(k * C, C)] = v.T.astype(BF16)

        for i in range(3):
            acc[i] = jnp.zeros((N, N), F32)

    pl.when(has_next)(activated)

    @pl.when(first)
    def _():
        cot_load.wait()

    @pl.when(first & has_below)
    def _():
        cot_low().wait_recv()

    @pl.when(first & has_above)
    def _():
        cot_high().wait_recv()

    @pl.when(has_prev)
    def _():
        @pl.loop(0, F // 2)
        def _(pair):
            t = F - 2 - 2 * pair
            arrive(t + 1)
            arrive(t)
            conv(t, 2)
            send(t + 1)
            send(t)

        if F % 2:
            arrive(0)
            conv(0, 1)
            send(0)

    pl.when(first)(activated)

    @pl.loop(0, F)
    def _(back_t):
        t = F - 1 - back_t

        @pl.when(s == 0)
        def _():
            arrive(t)

        if F % 2:
            @pl.when((t > 2) & (t % 2 == 1))
            def _():
                taps(t, 2, range(3))
        else:
            @pl.when(t > 2)
            def _():
                taps(t, 1, range(3))

        @pl.when(t == 2)
        def _():
            taps(2, 1, range(3))

        @pl.when(t == 1)
        def _():
            taps(1, 1, (1, 2))
            pair_sum(0)

        @pl.when(t == 0)
        def _():
            taps(0, 1, (2,))
            pair_sum(1)

    pair_sum(2)

    @pl.when(s == 0)
    def _():
        count = 3 if F % 3 == 0 else 1

        @pl.loop(0, F // count)
        def _(q):
            conv(q * count, count)


    for i in range(3):
        for zz in range(Z):
            @pl.when(z != zz)
            def _():
                chip_arrival(i, zz).wait_recv()
        total = r2[i, 0].astype(F32)
        for zz in range(1, Z):
            total = total + r2[i, zz].astype(F32)
        dw[pl.ds(9 * i, 9)] = total

    for i in range(3):
        pair_copy(i).wait_send()
        for zz in range(Z):
            @pl.when(z != zz)
            def _():
                chip_copy(i, zz).wait_send()

    @pl.when(first & has_above)
    def _():
        cot_low().wait_send()

    @pl.when(first & has_below)
    def _():
        cot_high().wait_send()

    @pl.when(has_prev)
    def _():
        @pl.loop(0, F)
        def _(t):
            rows_copy(t).wait_send()

    @pl.when(has_prev & has_above)
    def _():
        @pl.loop(0, F)
        def _(t):
            low_copy(t).wait_send()

    @pl.when(has_prev & has_below)
    def _():
        @pl.loop(0, F)
        def _(t):
            high_copy(t).wait_send()


def local(S, G, acts, kernels, cotangent):
    F, R, W, C = cotangent.shape
    share = C // G
    sp = -(-share // 16) * 16
    Z = G // 2
    M = R * W
    scale = 1.0 / math.sqrt(F * R * G * W)
    dma = pltpu.SemaphoreType.DMA
    dx, dw = pl.pallas_call(
        functools.partial(kernel, S, G, share),
        out_shape=(
            jax.ShapeDtypeStruct((F, R, W, C), BF16),
            jax.ShapeDtypeStruct((27, sp, C), F32),
        ),
        in_specs=[pl.BlockSpec(memory_space=pltpu.HBM)] * 3,
        out_specs=[pl.BlockSpec(memory_space=pltpu.VMEM)] * 2,
        scratch_shapes=[
            pltpu.VMEM((F, R, W, C), BF16),
            pltpu.VMEM((9, 3, C, C), BF16),
            pltpu.VMEM((F, R + 2, W, C), BF16),
            pltpu.VMEM((F + 2, M, 9 * C), BF16),
            pltpu.VMEM((9 * C, 3 * C), BF16),
            pltpu.VMEM((F, M, C), F32),
            pltpu.VMEM((F, 3 * C, M), BF16),
            pltpu.VMEM((3, 3 * C, 3 * C), F32),
            pltpu.VMEM((3, 2, Z, 9, sp, C), BF16),
            pltpu.VMEM((3, Z, 9, sp, C), BF16),
            pltpu.VMEM((3, Z, 9, sp, C), BF16),
            pltpu.VMEM((3, Z, 9, sp, C), BF16),
            dma((F,)), dma((F,)), dma((F,)), dma((F,)), dma((F,)), dma((F,)),
            dma((2,)), dma((2,)), dma((3,)),
            dma((3,)), dma((3,)), dma((3, Z)), dma((3, Z)),
        ],
        compiler_params=pltpu.CompilerParams(
            collective_id=0, has_side_effects=True, vmem_limit_bytes=64 * 2**20 - 2**18
        ),
        cost_estimate=pl.CostEstimate(
            flops=4 * 27 * F * M * C * C, bytes_accessed=4 * 27 * C * C, transcendentals=F * M * C
        ),
    )(acts[0], kernels[0].reshape(9, 3, C, C), cotangent)
    kernel_part = jnp.transpose(dw[:, :share], (1, 0, 2)) * scale
    return (dx[None], kernel_part[None])


def solution(mesh):
    return jax.shard_map(
        functools.partial(local, mesh.shape["section"], mesh.shape["dp"]),
        mesh=mesh,
        in_specs=(
            P("section", None, "dp", None, None),
            P("section", None, None, None, None, None),
            P(None, "dp", None, None),
        ),
        out_specs=(P("section", None, "dp", None, None), P("section", "dp", None, None)),
        check_vma=False,
    )
```
